128 devices in a mesh: dp: 4 (over z_lo, core), row: 8 (over y, z_hi), col: 4 (over x).
Axes of the slice: x: 4, y: 4, z: 4 (z_hi: 2, z_lo: 2; z = z_hi * 2 + z_lo), core: 2. Of those that a mesh axis runs over, the one named last changes fastest.
Arguments:
- layer_input: bfloat16 [4096, 8192], P(('dp', 'col'), 'row'), may hold values from -6 to 6
- hidden_grad: bfloat16 [4096, 14336], P(('dp', 'row'), 'col'), may hold values from -4 to 4
- gate_pre: bfloat16 [4096, 14336], P(('dp', 'row'), 'col'), may hold values from -10 to 10
- up_pre: bfloat16 [4096, 14336], P(('dp', 'row'), 'col'), may hold values from -6 to 6
- gate_weight: bfloat16 [8192, 14336], P('row', 'col'), may hold values from -0.0625 to 0.0625
- up_weight: bfloat16 [8192, 14336], P('row', 'col'), may hold values from -0.0625 to 0.0625
Outputs:
- input_grad: bfloat16 [4096, 8192], P(('dp', 'col'), 'row')
- gate_weight_grad: bfloat16 [8192, 14336], P(('row', 'dp'), 'col')
- up_weight_grad: bfloat16 [8192, 14336], P(('row', 'dp'), 'col')
The draws below stay inside these ranges and needn't reach their ends.
All inputs are finite; a program needn't handle non-finite values.
Results may differ from the reference program's by a relative error of at most 0.015.
Values may be sent and summed in bfloat16 or wider, within the bound.
No kernel may reach another device: no remote copies, remote signals or barrier semaphores. Data moves between devices by JAX's collectives and lax.ppermute only.
A program may use at most 256 MiB of HBM per device.

```python
import jax
import jax.numpy as jnp
from jax import lax

D = 8192
FF = 14336
TOK = 1024
TOKENS = 4096
N_DP = 4


def block_levels(own_key, extent, split, low, high):
    loudness, own = 1.0, jax.random.fold_in(own_key, 6)
    for dim, blocks in split:
        heights = jnp.exp(jax.random.uniform(jax.random.fold_in(own, dim), (blocks,), jnp.float32, low / len(split), high / len(split)))
        loudness = loudness * jnp.repeat(heights, extent[dim] // blocks).reshape([-1 if axis == dim else 1 for axis in range(len(extent))])
    return loudness


def scatter_about(stream_key, extent, scale, reach, shards=(), dtype=jnp.bfloat16):
    values = jax.random.normal(stream_key, extent, jnp.float32) * scale
    if len(shards) > 0:
        values = block_levels(stream_key, extent, shards, -0.22, 0.18) * values
    return jnp.clip(values, min=-reach, max=reach).astype(dtype)


def setup_inputs(seed: int = 0) -> dict:
    seeds = jax.random.split(jax.random.key(seed), 7)
    layer_input = scatter_about(seeds[0], (TOKENS, D), 1.0, 6.0, ((0, 16), (1, 8)))
    hidden_grad = scatter_about(seeds[1], (TOKENS, FF), 0.5, 4.0, ((0, 32), (1, 4)))
    gate_pre = scatter_about(seeds[2], (TOKENS, FF), 2.0, 10.0, ((0, 32), (1, 4)))
    up_pre = scatter_about(seeds[3], (TOKENS, FF), 1.0, 6.0, ((0, 32), (1, 4)))
    gate_weight = scatter_about(seeds[4], (D, FF), D ** -0.5, 0.0625, ((0, 8), (1, 4)))
    up_weight = scatter_about(seeds[5], (D, FF), D ** -0.5, 0.0625, ((0, 8), (1, 4)))
    return {"layer_input": layer_input, "hidden_grad": hidden_grad, "gate_pre": gate_pre, "up_pre": up_pre, "gate_weight": gate_weight, "up_weight": up_weight}


def reference(layer_input, hidden_grad, gate_pre, up_pre, gate_weight, up_weight):
    gate_value = gate_pre.astype(jnp.float32)
    sigmoid_gate = jax.nn.sigmoid(gate_value)
    grad_value = hidden_grad.astype(jnp.float32)
    gate_grad = (grad_value * up_pre.astype(jnp.float32) * sigmoid_gate * (1.0 + gate_value * (1.0 - sigmoid_gate))).astype(jnp.bfloat16)
    up_grad = (grad_value * gate_value * sigmoid_gate).astype(jnp.bfloat16)
    input_sum = jnp.dot(gate_grad, gate_weight.T, preferred_element_type=jnp.float32)
    input_sum = input_sum + jnp.dot(up_grad, up_weight.T, preferred_element_type=jnp.float32)
    input_grad = input_sum.astype(jnp.bfloat16)
    gate_total = jnp.zeros(gate_weight.shape, jnp.float32)
    up_total = jnp.zeros(up_weight.shape, jnp.float32)
    for group_index in range(N_DP):
        token_rows = layer_input[group_index * TOK:(group_index + 1) * TOK]
        gate_rows = gate_grad[group_index * TOK:(group_index + 1) * TOK]
        up_rows = up_grad[group_index * TOK:(group_index + 1) * TOK]
        gate_part = jnp.dot(token_rows.T, gate_rows, preferred_element_type=jnp.float32).astype(jnp.bfloat16)
        up_part = jnp.dot(token_rows.T, up_rows, preferred_element_type=jnp.float32).astype(jnp.bfloat16)
        gate_part, up_part = lax.optimization_barrier((gate_part, up_part))
        gate_total = gate_total + gate_part.astype(jnp.float32)
        up_total = up_total + up_part.astype(jnp.float32)
    inverse_groups = 1.0 / N_DP
    gate_weight_grad = (gate_total * inverse_groups).astype(jnp.bfloat16)
    up_weight_grad = (up_total * inverse_groups).astype(jnp.bfloat16)
    return input_grad, gate_weight_grad, up_weight_grad
```

```python
import jax
import jax.numpy as jnp
from jax import lax
from jax.sharding import PartitionSpec as P

CHUNKS = (512, 512, 512, 512, 512, 512, 512)
ROW_UP = [(i, (i + 2) % 8) for i in range(8)]
ROW_DOWN = [(i, (i - 2) % 8) for i in range(8)]
ROW_SWAP = [(i, i ^ 1) for i in range(8)]
COL_UP = [(i, (i + 1) % 4) for i in range(4)]
COL_DOWN = [(i, (i - 1) % 4) for i in range(4)]
COL_FAR = [(i, (i + 2) % 4) for i in range(4)]
CORE_SWAP = [(i, i ^ 1) for i in range(4)]
PAIR_SWAP = [(i, i ^ 2) for i in range(4)]


def after(value, *earlier):
    return lax.optimization_barrier((value, *earlier))[0]


def token_dot(first, second):
    return lax.dot_general(first, second, (((0,), (0,)), ((), ())), preferred_element_type=jnp.float32)


def hidden_dot(first, second):
    return lax.dot_general(first, second, (((1,), (1,)), ((), ())), preferred_element_type=jnp.float32)


def gate_up_grads(hidden_grad, gate_pre, up_pre):
    gate_value = gate_pre.astype(jnp.float32)
    sigmoid_gate = jax.nn.sigmoid(gate_value)
    grad_value = hidden_grad.astype(jnp.float32)
    gate_grad = (
        grad_value
        * up_pre.astype(jnp.float32)
        * sigmoid_gate
        * (1.0 + gate_value * (1.0 - sigmoid_gate))
    ).astype(jnp.bfloat16)
    up_grad = (grad_value * gate_value * sigmoid_gate).astype(jnp.bfloat16)
    return jnp.concatenate([gate_grad, up_grad], axis=1)


def body(layer_input, hidden_grad, gate_pre, up_pre, gate_weight, up_weight):
    row, col, dp = lax.axis_index("row"), lax.axis_index("col"), lax.axis_index("dp")
    y, z_hi = row // 2, row % 2
    tokens, width = layer_input.shape
    quarter = width // 4
    starts = [sum(CHUNKS[:i]) for i in range(len(CHUNKS))]
    count = len(CHUNKS)

    own = [
        gate_up_grads(*(a[:, s : s + w] for a in (hidden_grad, gate_pre, up_pre)))
        for s, w in zip(starts, CHUNKS)
    ]

    blocks = [
        layer_input,
        lax.ppermute(layer_input, "col", COL_DOWN),
        lax.ppermute(layer_input, "col", COL_FAR),
        lax.ppermute(layer_input, "col", COL_UP),
    ]
    ring = jnp.stack(blocks + blocks[:3])
    ring = lax.dynamic_slice_in_dim(ring, (y - col) % 4, 4, 0)
    ring = ring.reshape(4, 2, tokens // 2, width)
    ring = jnp.where(z_hi == 0, ring, ring[:, ::-1]).reshape(4 * tokens, width)
    part = lambda k: lax.dynamic_slice_in_dim(ring, (dp ^ k) * quarter, quarter, 1)
    input_send = jnp.concatenate([part(3), part(1)], axis=1)
    input_keep = jnp.concatenate([part(2), part(0)], axis=1)

    swapped, near, far = [None] * count, [None] * count, [None] * count
    for c in range(count):
        value = own[c] if c < 2 else after(own[c], swapped[c - 2])
        swapped[c] = lax.ppermute(value, "row", ROW_SWAP)
    for c in range(count):
        mine, other = own[c], swapped[c]
        if c >= 1:
            mine = after(mine, near[c - 1][0], near[c - 1][1])
            other = after(other, near[c - 1][2], near[c - 1][3])
        near[c] = (
            lax.ppermute(mine, "row", ROW_UP),
            lax.ppermute(mine, "row", ROW_DOWN),
            lax.ppermute(other, "row", ROW_UP),
            lax.ppermute(other, "row", ROW_DOWN),
        )
        far[c] = (
            lax.ppermute(near[c][0], "row", ROW_UP),
            lax.ppermute(near[c][3], "row", ROW_DOWN),
        )

    inverse_groups = 1.0 / lax.axis_size("dp")
    gate_out = jnp.zeros((quarter, gate_weight.shape[1]), jnp.bfloat16)
    up_out = jnp.zeros((quarter, gate_weight.shape[1]), jnp.bfloat16)
    input_sum = None
    for c in range(count):
        s, w = starts[c], CHUNKS[c]
        from_below, from_above, other_below, other_above = near[c]
        grads = jnp.concatenate(
            [own[c], swapped[c], from_above, other_above, far[c][0], far[c][1], from_below, other_below]
        )
        core_part = lax.ppermute(token_dot(input_send, grads).astype(jnp.bfloat16), "dp", CORE_SWAP)
        term = hidden_dot(grads[:, :w], gate_weight[:, s : s + w]) + hidden_dot(
            grads[:, w:], up_weight[:, s : s + w]
        )
        input_sum = term if input_sum is None else input_sum + term
        chip_part = token_dot(input_keep, grads) + core_part.astype(jnp.float32)
        pair_part = lax.ppermute(chip_part[:quarter].astype(jnp.bfloat16), "dp", PAIR_SWAP)
        total = chip_part[quarter:].astype(jnp.bfloat16).astype(jnp.float32) + pair_part.astype(jnp.float32)
        total = (total * inverse_groups).astype(jnp.bfloat16)
        gate_out = lax.dynamic_update_slice(gate_out, total[:, :w], (0, s))
        up_out = lax.dynamic_update_slice(up_out, total[:, w:], (0, s))

    input_part = input_sum.astype(jnp.bfloat16)
    block = lambda k: lax.dynamic_slice_in_dim(input_part, ((col + k - y) % 4) * tokens, tokens, 0)
    pieces = (
        block(0),
        lax.ppermute(block(1), "col", COL_UP),
        lax.ppermute(block(2), "col", COL_FAR),
        lax.ppermute(block(3), "col", COL_DOWN),
    )
    input_grad = sum(p.astype(jnp.float32) for p in pieces)
    halves = input_grad.reshape(2, tokens // 2, width)
    input_grad = jnp.where(z_hi == 0, halves, halves[::-1]).reshape(tokens, width).astype(jnp.bfloat16)
    return input_grad, gate_out, up_out


def solution(mesh):
    return jax.shard_map(
        body,
        mesh=mesh,
        in_specs=(
            P(("dp", "col"), "row"),
            P(("dp", "row"), "col"),
            P(("dp", "row"), "col"),
            P(("dp", "row"), "col"),
            P("row", "col"),
            P("row", "col"),
        ),
        out_specs=(P(("dp", "col"), "row"), P(("row", "dp"), "col"), P(("row", "dp"), "col")),
        check_vma=False,
    )
```

```python
import jax
import jax.numpy as jnp
from jax import lax
from jax.experimental import pallas as pl
from jax.experimental.pallas import tpu as pltpu
from jax.sharding import PartitionSpec as P

CHUNKS = ((3072, 512, False), (0, 1024, True), (1024, 1024, False), (2048, 1024, False))
SAME_Z = [[0, 2, 4, 6], [1, 3, 5, 7]]
ROW_UP = [(i, (i + 2) % 8) for i in range(8)]
ROW_DOWN = [(i, (i - 2) % 8) for i in range(8)]
ROW_SWAP = [(i, i ^ 1) for i in range(8)]
COL_UP = [(i, (i + 1) % 4) for i in range(4)]
COL_DOWN = [(i, (i - 1) % 4) for i in range(4)]
COL_FAR = [(i, (i + 2) % 4) for i in range(4)]
CORE_SWAP = [(i, i ^ 1) for i in range(4)]
PAIR_SWAP = [(i, i ^ 2) for i in range(4)]


TILES = 2
VMEM_BYTES = 40 * 1024 * 1024
NO_COST = pl.CostEstimate(flops=0, bytes_accessed=0, transcendentals=0)


def after(value, *earlier):
    return lax.optimization_barrier((value, *earlier))[0]


def after_all(values, *earlier):
    return list(lax.optimization_barrier((*values, *earlier)))[: len(values)]


def params():
    return pltpu.CompilerParams(dimension_semantics=("arbitrary",), vmem_limit_bytes=VMEM_BYTES)


def gate_up_grads(hidden_grad, gate_pre, up_pre):
    gate_value = gate_pre.astype(jnp.float32)
    sigmoid_gate = jax.nn.sigmoid(gate_value)
    grad_value = hidden_grad.astype(jnp.float32)
    gate_grad = (
        grad_value
        * up_pre.astype(jnp.float32)
        * sigmoid_gate
        * (1.0 + gate_value * (1.0 - sigmoid_gate))
    ).astype(jnp.bfloat16)
    up_grad = (grad_value * gate_value * sigmoid_gate).astype(jnp.bfloat16)
    return jnp.concatenate([gate_grad, up_grad], axis=1)


def order_input(group_input, row, dp):
    tokens, width = group_input.shape
    half, quarter = tokens // 8, width // 4
    picks = (jnp.arange(8, dtype=jnp.int32) ^ (row % 2)).astype(jnp.int32)
    parts = (dp ^ jnp.array([3, 1, 2, 0], jnp.int32)).astype(jnp.int32)

    def kernel(picks_ref, parts_ref, in_ref, out_ref):
        for i in range(8):
            rows = pl.ds(pl.multiple_of(picks_ref[i] * half, half), half)
            for k in range(4):
                columns = pl.ds(pl.multiple_of(parts_ref[k] * quarter, quarter), quarter)
                out_ref[k * quarter : (k + 1) * quarter, i * half : (i + 1) * half] = in_ref[rows, columns].T

    return pl.pallas_call(
        kernel,
        out_shape=jax.ShapeDtypeStruct((width, tokens), group_input.dtype),
        grid_spec=pltpu.PrefetchScalarGridSpec(
            num_scalar_prefetch=2,
            grid=(1,),
            in_specs=[pl.BlockSpec((tokens, width), lambda i, *_: (0, 0))],
            out_specs=pl.BlockSpec((width, tokens), lambda i, *_: (0, 0)),
        ),
        compiler_params=params(),
        cost_estimate=NO_COST,
        name="order_input",
    )(picks, parts, group_input)


def join_rows(places, pieces):
    rows, columns = pieces[0].shape
    count = len(pieces)

    def kernel(places_ref, *refs):
        out_ref, sems = refs[count], refs[count + 1]
        copies = []
        for k in range(count):
            at = pl.ds(pl.multiple_of(places_ref[k] * rows, rows), rows)
            copies.append(pltpu.make_async_copy(refs[k], out_ref.at[at, :], sems.at[k]))
        for copy in copies:
            copy.start()
        for copy in copies:
            copy.wait()

    return pl.pallas_call(
        kernel,
        out_shape=jax.ShapeDtypeStruct((rows * count, columns), pieces[0].dtype),
        grid_spec=pltpu.PrefetchScalarGridSpec(
            num_scalar_prefetch=1,
            grid=(1,),
            in_specs=[pl.BlockSpec(memory_space=pl.ANY)] * count,
            out_specs=pl.BlockSpec((rows * count, columns), lambda i, places: (0, 0)),
            scratch_shapes=[pltpu.SemaphoreType.DMA((count,))],
        ),
        compiler_params=params(),
        cost_estimate=NO_COST,
        name="join_rows",
    )(places, *pieces)


def chunk_grads(places, pieces, input_columns, gate_weight, up_weight, start, total, last):
    count = len(pieces)
    rows, hidden = pieces[0].shape
    tokens = rows * count
    width = (input_columns if gate_weight is None else gate_weight).shape[0]
    w = hidden // 2
    tile = width // TILES
    half = TILES // 2
    column = start // w
    block = tokens // 4
    with_weight, with_input = input_columns is not None, gate_weight is not None

    def kernel(places_ref, *refs):
        refs = list(refs)
        take = lambda k: [refs.pop(0) for _ in range(k)]
        piece_refs = take(count)
        input_refs = take(1) if with_weight else []
        weight_refs = take(2) if with_input else []
        total_refs = take(1) if total is not None else []
        part_refs = take(2) if with_weight else []
        sum_refs = take(4 if last else 1) if with_input else []
        if count > 1:
            rows_ref = refs.pop(0)

            @pl.when(pl.program_id(0) == 0)
            def _():
                for k in range(count):
                    rows_ref[pl.ds(pl.multiple_of(places_ref[k] * rows, rows), rows), :] = piece_refs[k][...]
        else:
            rows_ref = piece_refs[0]

        if with_weight:
            part = jnp.dot(input_refs[0][...], rows_ref[...], preferred_element_type=jnp.float32).astype(jnp.bfloat16)

            @pl.when(pl.program_id(0) < half)
            def _():
                part_refs[0][...] = part

            @pl.when(pl.program_id(0) >= half)
            def _():
                part_refs[1][...] = part

        if with_input:
            across = (((1,), (1,)), ((), ()))
            term = lax.dot_general(rows_ref[:, :w], weight_refs[0][...], across, preferred_element_type=jnp.float32)
            term += lax.dot_general(rows_ref[:, w:], weight_refs[1][...], across, preferred_element_type=jnp.float32)
            if total_refs:
                term += total_refs[0][...]
            if last:
                sum_ref = refs.pop(0)
                sum_ref[...] = term
                for k in range(4):
                    at = pl.multiple_of(places_ref[8 + k] * block, block)
                    sum_refs[k][...] = sum_ref[pl.ds(at, block), :].astype(jnp.bfloat16)
            else:
                sum_refs[0][...] = term

    in_specs = [pl.BlockSpec((rows, hidden), lambda i, _: (0, 0), pipeline_mode=pl.Buffered(1))] * count
    operands = [*pieces]
    out_shape, out_specs, scratch = [], [], []
    if count > 1:
        scratch.append(pltpu.VMEM((tokens, hidden), jnp.bfloat16))
    if with_weight:
        in_specs.append(pl.BlockSpec((tile, tokens), lambda i, _: (i, 0)))
        operands.append(input_columns)
        out_shape += [jax.ShapeDtypeStruct((width // 2, hidden), jnp.bfloat16)] * 2
        out_specs += [
            pl.BlockSpec((tile, hidden), lambda i, _: (jnp.minimum(i, half - 1), 0)),
            pl.BlockSpec((tile, hidden), lambda i, _: (jnp.maximum(i - half, 0), 0)),
        ]
    if with_input:
        in_specs += [pl.BlockSpec((tile, w), lambda i, _: (i, column))] * 2
        operands += [gate_weight, up_weight]
        if total is not None:
            in_specs.append(pl.BlockSpec((tokens, tile), lambda i, _: (0, i)))
            operands.append(total)
        if last:
            out_shape += [jax.ShapeDtypeStruct((block, width), jnp.bfloat16)] * 4
            out_specs += [pl.BlockSpec((block, tile), lambda i, _: (0, i))] * 4
            scratch.append(pltpu.VMEM((tokens, tile), jnp.float32))
        else:
            out_shape.append(jax.ShapeDtypeStruct((tokens, width), jnp.float32))
            out_specs.append(pl.BlockSpec((tokens, tile), lambda i, _: (0, i)))
    return pl.pallas_call(
        kernel,
        out_shape=tuple(out_shape),
        grid_spec=pltpu.PrefetchScalarGridSpec(
            num_scalar_prefetch=1, grid=(TILES,), in_specs=in_specs, out_specs=tuple(out_specs), scratch_shapes=scratch
        ),
        compiler_params=params(),
        cost_estimate=NO_COST,
        name="chunk_grads",
    )(places, *operands)


def body(layer_input, hidden_grad, gate_pre, up_pre, gate_weight, up_weight):
    row, col, dp = lax.axis_index("row"), lax.axis_index("col"), lax.axis_index("dp")
    y, z_hi = row // 2, row % 2
    tokens, width = layer_input.shape
    quarter = width // 4
    count = len(CHUNKS)
    steps = jnp.arange(4, dtype=jnp.int32)
    blocks = (y + steps) % 4
    places = jnp.concatenate([jnp.stack([2 * blocks, 2 * blocks + 1], axis=1).reshape(8), (col + steps) % 4])
    places = places.astype(jnp.int32)

    swap = lambda value: lax.ppermute(value, "row", ROW_SWAP)
    up = lambda value: lax.ppermute(value, "row", ROW_UP)
    down = lambda value: lax.ppermute(value, "row", ROW_DOWN)
    gather = lambda value: lax.all_gather(value, "row", axis=0, tiled=True, axis_index_groups=SAME_Z)
    own, other, below, above, other_below, other_above, far, other_far, rows = ([None] * count for _ in range(9))

    def grads_of(c):
        s, w, _ = CHUNKS[c]
        return gate_up_grads(*(a[:, s : s + w] for a in (hidden_grad, gate_pre, up_pre)))

    group_input = lax.all_gather(layer_input, "col", axis=0, tiled=True)
    own[0] = grads_of(0)
    other[0] = swap(own[0])
    below[0], above[0] = up(own[0]), down(own[0])
    hidden_grad = after(hidden_grad, own[0])
    for c in range(1, count):
        own[c] = grads_of(c)
    below[2], above[2] = up(own[2]), down(own[2])
    first = (below[0], above[0], other[0])
    other[1] = swap(after(own[1], *first))
    other_0 = after(other[0], *first)
    other_below[0], other_above[0] = up(other_0), down(other_0)
    far[0] = up(after(below[0], *first))
    other[2] = swap(after(own[2], below[2]))
    other[3] = swap(after(own[3], other[1]))
    second = (below[2], above[2], other_below[0], other_above[0])
    other_far[0] = down(after(other_above[0], *second))
    far[2] = up(after(below[2], *second))
    whole_1 = join_rows(steps[:2], after_all([own[1], other[1]], *second))
    rows[1] = gather(whole_1)
    third = (far[0], other_far[0], other[2])
    input_columns = order_input(after(group_input, *third, whole_1), row, dp)
    other_below[2], other_above[2] = up(other[2]), down(other[2])
    own_3 = after(own[3], other_below[2], other_above[2])
    below[3], above[3] = up(own_3), down(own_3)
    before = [third, (other_below[2], other_above[2]), (), ()]

    inverse_groups = 1.0 / lax.axis_size("dp")
    gate_out = jnp.zeros((quarter, gate_weight.shape[1]), jnp.bfloat16)
    up_out = jnp.zeros((quarter, gate_weight.shape[1]), jnp.bfloat16)
    total = None
    chip_send, pair_parts = [None] * count, [None] * count
    for c, (s, w, gathered) in enumerate(CHUNKS):
        earlier = [*before[c]]
        if c >= 1:
            earlier += [pair_parts[c - 1], total]
        if c == 1:
            other_far[2] = down(after(other_above[2], chip_send[0]))
            other_3 = after(other[3], below[3], other_far[2])
            other_below[3], other_above[3] = up(other_3), down(other_3)
            far[3], other_far[3] = up(below[3]), down(other_above[3])
            before[2:] = [(above[3], other_below[3], other_above[3]), (far[3], other_far[3])]
        pieces = [rows[c]] if gathered else [
            own[c], other[c], above[c], other_above[c], far[c], other_far[c], below[c], other_below[c]
        ]
        if c == count - 1:
            shares = chunk_grads(
                places, after_all(pieces, chip_send[c - 1], total), None, gate_weight, up_weight, s, total, True
            )
            mine, next_one, across, last_one = shares
            shares = (
                mine,
                lax.ppermute(next_one, "col", COL_UP),
                lax.ppermute(last_one, "col", COL_DOWN),
                lax.ppermute(across, "col", COL_FAR),
            )
            earlier += shares[:1]
        pieces = after_all(pieces, *earlier)
        send, keep = chunk_grads(places, pieces, input_columns, None, None, s, None, False)
        core_part = lax.ppermute(send, "dp", CORE_SWAP)
        chip_send[c] = (keep[:quarter].astype(jnp.float32) + core_part[:quarter].astype(jnp.float32)).astype(jnp.bfloat16)
        pair_part = pair_parts[c] = lax.ppermute(chip_send[c], "dp", PAIR_SWAP)
        if c < count - 1:
            pieces = after_all(pieces, chip_send[c])
            (total,) = chunk_grads(places, pieces, None, gate_weight, up_weight, s, total, False)

        def finish(columns):
            value = keep[quarter:, columns].astype(jnp.float32) + core_part[quarter:, columns].astype(jnp.float32)
            return ((value + pair_part[:, columns].astype(jnp.float32)) * inverse_groups).astype(jnp.bfloat16)

        gate_out = lax.dynamic_update_slice(gate_out, finish(slice(0, w)), (0, s))
        up_out = lax.dynamic_update_slice(up_out, finish(slice(w, 2 * w)), (0, s))

    input_grad = sum(share.astype(jnp.float32) for share in shares)
    halves = input_grad.reshape(2, tokens // 2, width)
    input_grad = jnp.where(z_hi == 0, halves, halves[::-1]).reshape(tokens, width).astype(jnp.bfloat16)
    return input_grad, gate_out, up_out


def solution(mesh):
    return jax.shard_map(
        body,
        mesh=mesh,
        in_specs=(
            P(("dp", "col"), "row"),
            P(("dp", "row"), "col"),
            P(("dp", "row"), "col"),
            P(("dp", "row"), "col"),
            P("row", "col"),
            P("row", "col"),
        ),
        out_specs=(P(("dp", "col"), "row"), P(("row", "dp"), "col"), P(("row", "dp"), "col")),
        check_vma=False,
    )
```

```python
import jax
import jax.numpy as jnp
from jax import lax
from jax.experimental import pallas as pl
from jax.experimental.pallas import tpu as pltpu
from jax.sharding import PartitionSpec as P

CHUNKS = ((3072, 512, False), (0, 1024, True), (1024, 1024, False), (2048, 1024, False))
SAME_Z = [[0, 2, 4, 6], [1, 3, 5, 7]]
ROW_UP = [(i, (i + 2) % 8) for i in range(8)]
ROW_DOWN = [(i, (i - 2) % 8) for i in range(8)]
ROW_SWAP = [(i, i ^ 1) for i in range(8)]
CORE_SWAP = [(i, i ^ 1) for i in range(4)]
PAIR_SWAP = [(i, i ^ 2) for i in range(4)]


TILES = 2
VMEM_BYTES = 40 * 1024 * 1024
NO_COST = pl.CostEstimate(flops=0, bytes_accessed=0, transcendentals=0)


def after(value, *earlier):
    return lax.optimization_barrier((value, *earlier))[0]


def after_all(values, *earlier):
    return list(lax.optimization_barrier((*values, *earlier)))[: len(values)]


def params():
    return pltpu.CompilerParams(dimension_semantics=("arbitrary",), vmem_limit_bytes=VMEM_BYTES)


def gate_up_grads(hidden_grad, gate_pre, up_pre):
    gate_value = gate_pre.astype(jnp.float32)
    sigmoid_gate = jax.nn.sigmoid(gate_value)
    grad_value = hidden_grad.astype(jnp.float32)
    gate_grad = (
        grad_value
        * up_pre.astype(jnp.float32)
        * sigmoid_gate
        * (1.0 + gate_value * (1.0 - sigmoid_gate))
    ).astype(jnp.bfloat16)
    up_grad = (grad_value * gate_value * sigmoid_gate).astype(jnp.bfloat16)
    return jnp.concatenate([gate_grad, up_grad], axis=1)


def order_input(group_input, row, dp):
    tokens, width = group_input.shape
    half, quarter = tokens // 8, width // 4
    picks = (jnp.arange(8, dtype=jnp.int32) ^ (row % 2)).astype(jnp.int32)
    parts = (dp ^ jnp.array([3, 1, 2, 0], jnp.int32)).astype(jnp.int32)

    def kernel(picks_ref, parts_ref, in_ref, out_ref):
        for i in range(8):
            rows = pl.ds(pl.multiple_of(picks_ref[i] * half, half), half)
            for k in range(4):
                columns = pl.ds(pl.multiple_of(parts_ref[k] * quarter, quarter), quarter)
                out_ref[k * quarter : (k + 1) * quarter, i * half : (i + 1) * half] = in_ref[rows, columns].T

    return pl.pallas_call(
        kernel,
        out_shape=jax.ShapeDtypeStruct((width, tokens), group_input.dtype),
        grid_spec=pltpu.PrefetchScalarGridSpec(
            num_scalar_prefetch=2,
            grid=(1,),
            in_specs=[pl.BlockSpec((tokens, width), lambda i, *_: (0, 0))],
            out_specs=pl.BlockSpec((width, tokens), lambda i, *_: (0, 0)),
        ),
        compiler_params=params(),
        cost_estimate=NO_COST,
        name="order_input",
    )(picks, parts, group_input)


def join_rows(places, pieces):
    rows, columns = pieces[0].shape
    count = len(pieces)

    def kernel(places_ref, *refs):
        out_ref, sems = refs[count], refs[count + 1]
        copies = []
        for k in range(count):
            at = pl.ds(pl.multiple_of(places_ref[k] * rows, rows), rows)
            copies.append(pltpu.make_async_copy(refs[k], out_ref.at[at, :], sems.at[k]))
        for copy in copies:
            copy.start()
        for copy in copies:
            copy.wait()

    return pl.pallas_call(
        kernel,
        out_shape=jax.ShapeDtypeStruct((rows * count, columns), pieces[0].dtype),
        grid_spec=pltpu.PrefetchScalarGridSpec(
            num_scalar_prefetch=1,
            grid=(1,),
            in_specs=[pl.BlockSpec(memory_space=pl.ANY)] * count,
            out_specs=pl.BlockSpec((rows * count, columns), lambda i, places: (0, 0)),
            scratch_shapes=[pltpu.SemaphoreType.DMA((count,))],
        ),
        compiler_params=params(),
        cost_estimate=NO_COST,
        name="join_rows",
    )(places, *pieces)


def chunk_grads(places, pieces, input_columns, gate_weight, up_weight, start, total, last):
    count = len(pieces)
    rows, hidden = pieces[0].shape
    tokens = rows * count
    width = (input_columns if gate_weight is None else gate_weight).shape[0]
    w = hidden // 2
    tile = width // TILES
    half = TILES // 2
    column = start // w
    with_weight, with_input = input_columns is not None, gate_weight is not None

    def kernel(places_ref, *refs):
        refs = list(refs)
        take = lambda k: [refs.pop(0) for _ in range(k)]
        piece_refs = take(count)
        input_refs = take(1) if with_weight else []
        weight_refs = take(2) if with_input else []
        total_refs = take(1) if total is not None else []
        part_refs = take(2) if with_weight else []
        sum_refs = take(1) if with_input else []
        if count > 1:
            rows_ref = refs.pop(0)

            @pl.when(pl.program_id(0) == 0)
            def _():
                for k in range(count):
                    rows_ref[pl.ds(pl.multiple_of(places_ref[k] * rows, rows), rows), :] = piece_refs[k][...]
        else:
            rows_ref = piece_refs[0]

        if with_weight:
            part = jnp.dot(input_refs[0][...], rows_ref[...], preferred_element_type=jnp.float32).astype(jnp.bfloat16)

            @pl.when(pl.program_id(0) < half)
            def _():
                part_refs[0][...] = part

            @pl.when(pl.program_id(0) >= half)
            def _():
                part_refs[1][...] = part

        if with_input:
            across = (((1,), (1,)), ((), ()))
            term = lax.dot_general(rows_ref[:, :w], weight_refs[0][...], across, preferred_element_type=jnp.float32)
            term += lax.dot_general(rows_ref[:, w:], weight_refs[1][...], across, preferred_element_type=jnp.float32)
            if total_refs:
                term += total_refs[0][...]
            sum_refs[0][...] = term.astype(sum_refs[0].dtype)

    in_specs = [pl.BlockSpec((rows, hidden), lambda i, _: (0, 0), pipeline_mode=pl.Buffered(1))] * count
    operands = [*pieces]
    out_shape, out_specs, scratch = [], [], []
    if count > 1:
        scratch.append(pltpu.VMEM((tokens, hidden), jnp.bfloat16))
    if with_weight:
        in_specs.append(pl.BlockSpec((tile, tokens), lambda i, _: (i, 0)))
        operands.append(input_columns)
        out_shape += [jax.ShapeDtypeStruct((width // 2, hidden), jnp.bfloat16)] * 2
        out_specs += [
            pl.BlockSpec((tile, hidden), lambda i, _: (jnp.minimum(i, half - 1), 0)),
            pl.BlockSpec((tile, hidden), lambda i, _: (jnp.maximum(i - half, 0), 0)),
        ]
    if with_input:
        in_specs += [pl.BlockSpec((tile, w), lambda i, _: (i, column))] * 2
        operands += [gate_weight, up_weight]
        if total is not None:
            in_specs.append(pl.BlockSpec((tokens, tile), lambda i, _: (0, i)))
            operands.append(total)
        out_shape.append(jax.ShapeDtypeStruct((tokens, width), jnp.bfloat16 if last else jnp.float32))
        out_specs.append(pl.BlockSpec((tokens, tile), lambda i, _: (0, i)))
    return pl.pallas_call(
        kernel,
        out_shape=tuple(out_shape),
        grid_spec=pltpu.PrefetchScalarGridSpec(
            num_scalar_prefetch=1, grid=(TILES,), in_specs=in_specs, out_specs=tuple(out_specs), scratch_shapes=scratch
        ),
        compiler_params=params(),
        cost_estimate=NO_COST,
        name="chunk_grads",
    )(places, *operands)


def body(layer_input, hidden_grad, gate_pre, up_pre, gate_weight, up_weight):
    row, dp = lax.axis_index("row"), lax.axis_index("dp")
    y, z_hi = row // 2, row % 2
    tokens, width = layer_input.shape
    quarter = width // 4
    count = len(CHUNKS)
    steps = jnp.arange(4, dtype=jnp.int32)
    blocks = (y + steps) % 4
    places = jnp.stack([2 * blocks, 2 * blocks + 1], axis=1).reshape(8).astype(jnp.int32)

    swap = lambda value: lax.ppermute(value, "row", ROW_SWAP)
    up = lambda value: lax.ppermute(value, "row", ROW_UP)
    down = lambda value: lax.ppermute(value, "row", ROW_DOWN)
    gather = lambda value: lax.all_gather(value, "row", axis=0, tiled=True, axis_index_groups=SAME_Z)
    own, other, below, above, other_below, other_above, far, other_far, rows = ([None] * count for _ in range(9))

    def grads_of(c):
        s, w, _ = CHUNKS[c]
        return gate_up_grads(*(a[:, s : s + w] for a in (hidden_grad, gate_pre, up_pre)))

    group_input = lax.all_gather(layer_input, "col", axis=0, tiled=True)
    own[0] = grads_of(0)
    other[0] = swap(own[0])
    below[0], above[0] = up(own[0]), down(own[0])
    hidden_grad = after(hidden_grad, own[0])
    for c in range(1, count):
        own[c] = grads_of(c)
    below[2], above[2] = up(own[2]), down(own[2])
    first = (below[0], above[0], other[0])
    other[1] = swap(after(own[1], *first))
    other_0 = after(other[0], *first)
    other_below[0], other_above[0] = up(other_0), down(other_0)
    far[0] = up(after(below[0], *first))
    other[2] = swap(after(own[2], below[2]))
    other[3] = swap(after(own[3], other[1]))
    second = (below[2], above[2], other_below[0], other_above[0])
    other_far[0] = down(after(other_above[0], *second))
    far[2] = up(after(below[2], *second))
    whole_1 = join_rows(steps[:2], after_all([own[1], other[1]], *second))
    rows[1] = gather(whole_1)
    third = (far[0], other_far[0], other[2], other[3])
    input_columns = order_input(after(group_input, *third, whole_1), row, dp)
    other_below[2], other_above[2] = up(other[2]), down(other[2])
    own_3 = after(own[3], other_below[2], other_above[2])
    below[3], above[3] = up(own_3), down(own_3)
    before = [third, (other_below[2], other_above[2]), (), ()]

    inverse_groups = 1.0 / lax.axis_size("dp")
    gate_out = jnp.zeros((quarter, gate_weight.shape[1]), jnp.bfloat16)
    up_out = jnp.zeros((quarter, gate_weight.shape[1]), jnp.bfloat16)
    total = None
    chip_send, pair_parts, finishes = [None] * count, [None] * count, [None] * count
    for c, (s, w, gathered) in enumerate(CHUNKS):
        earlier = [*before[c]]
        if c >= 1:
            earlier += [pair_parts[c - 1], total]
        if c == 1:
            other_far[2] = down(after(other_above[2], chip_send[0]))
            other_3 = after(other[3], below[3], other_far[2])
            other_below[3], other_above[3] = up(other_3), down(other_3)
            far[3], other_far[3] = up(below[3]), down(other_above[3])
            before[2:] = [(above[3], other_below[3], other_above[3]), (far[3], other_far[3])]
        pieces = [rows[c]] if gathered else [
            own[c], other[c], above[c], other_above[c], far[c], other_far[c], below[c], other_below[c]
        ]
        if c == count - 1:
            (input_part,) = chunk_grads(
                places, after_all(pieces, chip_send[c - 1], total), None, gate_weight, up_weight, s, total, True
            )
            gate_out, up_out = after_all([gate_out, up_out], total)
            earlier += [input_part, gate_out, up_out]
        pieces = after_all(pieces, *earlier)
        send, keep = chunk_grads(places, pieces, input_columns, None, None, s, None, False)
        core_part = lax.ppermute(send, "dp", CORE_SWAP)
        chip_send[c] = (keep[:quarter].astype(jnp.float32) + core_part[:quarter].astype(jnp.float32)).astype(jnp.bfloat16)
        pair_part = pair_parts[c] = lax.ppermute(chip_send[c], "dp", PAIR_SWAP)
        if c < count - 1:
            pieces = after_all(pieces, chip_send[c])
            (total,) = chunk_grads(places, pieces, None, gate_weight, up_weight, s, total, False)

        def finish(columns, keep=keep, core_part=core_part, pair_part=pair_part):
            value = keep[quarter:, columns].astype(jnp.float32) + core_part[quarter:, columns].astype(jnp.float32)
            return ((value + pair_part[:, columns].astype(jnp.float32)) * inverse_groups).astype(jnp.bfloat16)

        finishes[c] = finish
        for k in ([c - 1] if c else []) + ([c] if c == count - 1 else []):
            start, hidden = CHUNKS[k][:2]
            gate_out = lax.dynamic_update_slice(gate_out, finishes[k](slice(0, hidden)), (0, start))
            up_out = lax.dynamic_update_slice(up_out, finishes[k](slice(hidden, 2 * hidden)), (0, start))

    input_grad = lax.psum_scatter(input_part, "col", scatter_dimension=0, tiled=True)
    halves = input_grad.reshape(2, tokens // 2, width)
    input_grad = jnp.where(z_hi == 0, halves, halves[::-1]).reshape(tokens, width)
    return input_grad, gate_out, up_out


def solution(mesh):
    return jax.shard_map(
        body,
        mesh=mesh,
        in_specs=(
            P(("dp", "col"), "row"),
            P(("dp", "row"), "col"),
            P(("dp", "row"), "col"),
            P(("dp", "row"), "col"),
            P("row", "col"),
            P("row", "col"),
        ),
        out_specs=(P(("dp", "col"), "row"), P(("row", "dp"), "col"), P(("row", "dp"), "col")),
        check_vma=False,
    )
```

```python
import jax
import jax.numpy as jnp
from jax import lax
from jax.experimental import pallas as pl
from jax.experimental.pallas import tpu as pltpu
from jax.sharding import PartitionSpec as P

CHUNKS = ((3072, 512, False), (0, 1024, True), (1024, 1024, False), (2048, 1024, False))
SAME_Z = [[0, 2, 4, 6], [1, 3, 5, 7]]
ROW_UP = [(i, (i + 2) % 8) for i in range(8)]
ROW_DOWN = [(i, (i - 2) % 8) for i in range(8)]
ROW_SWAP = [(i, i ^ 1) for i in range(8)]
CORE_SWAP = [(i, i ^ 1) for i in range(4)]
PAIR_SWAP = [(i, i ^ 2) for i in range(4)]


TILES = 2
VMEM_BYTES = 40 * 1024 * 1024
NO_COST = pl.CostEstimate(flops=0, bytes_accessed=0, transcendentals=0)


def after(value, *earlier):
    return lax.optimization_barrier((value, *earlier))[0]


def after_all(values, *earlier):
    return list(lax.optimization_barrier((*values, *earlier)))[: len(values)]


def params():
    return pltpu.CompilerParams(dimension_semantics=("arbitrary",), vmem_limit_bytes=VMEM_BYTES)


def gate_up_grads(hidden_grad, gate_pre, up_pre):
    gate_value = gate_pre.astype(jnp.float32)
    sigmoid_gate = jax.nn.sigmoid(gate_value)
    grad_value = hidden_grad.astype(jnp.float32)
    gate_grad = (
        grad_value
        * up_pre.astype(jnp.float32)
        * sigmoid_gate
        * (1.0 + gate_value * (1.0 - sigmoid_gate))
    ).astype(jnp.bfloat16)
    up_grad = (grad_value * gate_value * sigmoid_gate).astype(jnp.bfloat16)
    return jnp.concatenate([gate_grad, up_grad], axis=1)


def order_input(group_input, row, dp):
    tokens, width = group_input.shape
    half, quarter = tokens // 8, width // 4
    picks = (jnp.arange(8, dtype=jnp.int32) ^ (row % 2)).astype(jnp.int32)
    parts = (dp ^ jnp.array([3, 1, 2, 0], jnp.int32)).astype(jnp.int32)

    def kernel(picks_ref, parts_ref, in_ref, out_ref):
        for i in range(8):
            rows = pl.ds(pl.multiple_of(picks_ref[i] * half, half), half)
            for k in range(4):
                columns = pl.ds(pl.multiple_of(parts_ref[k] * quarter, quarter), quarter)
                out_ref[k * quarter : (k + 1) * quarter, i * half : (i + 1) * half] = in_ref[rows, columns].T

    return pl.pallas_call(
        kernel,
        out_shape=jax.ShapeDtypeStruct((width, tokens), group_input.dtype),
        grid_spec=pltpu.PrefetchScalarGridSpec(
            num_scalar_prefetch=2,
            grid=(1,),
            in_specs=[pl.BlockSpec((tokens, width), lambda i, *_: (0, 0))],
            out_specs=pl.BlockSpec((width, tokens), lambda i, *_: (0, 0)),
        ),
        compiler_params=params(),
        cost_estimate=NO_COST,
        name="order_input",
    )(picks, parts, group_input)


def join_rows(places, pieces):
    rows, columns = pieces[0].shape
    count = len(pieces)

    def kernel(places_ref, *refs):
        out_ref, sems = refs[count], refs[count + 1]
        copies = []
        for k in range(count):
            at = pl.ds(pl.multiple_of(places_ref[k] * rows, rows), rows)
            copies.append(pltpu.make_async_copy(refs[k], out_ref.at[at, :], sems.at[k]))
        for copy in copies:
            copy.start()
        for copy in copies:
            copy.wait()

    return pl.pallas_call(
        kernel,
        out_shape=jax.ShapeDtypeStruct((rows * count, columns), pieces[0].dtype),
        grid_spec=pltpu.PrefetchScalarGridSpec(
            num_scalar_prefetch=1,
            grid=(1,),
            in_specs=[pl.BlockSpec(memory_space=pl.ANY)] * count,
            out_specs=pl.BlockSpec((rows * count, columns), lambda i, places: (0, 0)),
            scratch_shapes=[pltpu.SemaphoreType.DMA((count,))],
        ),
        compiler_params=params(),
        cost_estimate=NO_COST,
        name="join_rows",
    )(places, *pieces)


def chunk_grads(places, pieces, input_columns, gate_weight, up_weight, start, total, last):
    count = len(pieces)
    rows, hidden = pieces[0].shape
    tokens = rows * count
    width = (input_columns if gate_weight is None else gate_weight).shape[0]
    w = hidden // 2
    tile = width // TILES
    column = start // w
    with_weight, with_input = input_columns is not None, gate_weight is not None

    def kernel(places_ref, *refs):
        refs = list(refs)
        take = lambda k: [refs.pop(0) for _ in range(k)]
        piece_refs = take(count)
        input_refs = take(1) if with_weight else []
        weight_refs = take(2) if with_input else []
        total_refs = take(1) if total is not None else []
        part_refs = take(3) if with_weight else []
        sum_refs = take(1) if with_input else []
        if count > 1:
            rows_ref = refs.pop(0)

            @pl.when(pl.program_id(0) == 0)
            def _():
                for k in range(count):
                    rows_ref[pl.ds(pl.multiple_of(places_ref[k] * rows, rows), rows), :] = piece_refs[k][...]
        else:
            rows_ref = piece_refs[0]

        if with_weight:
            part = jnp.dot(input_refs[0][...], rows_ref[...], preferred_element_type=jnp.float32).astype(jnp.bfloat16)

            @pl.when(pl.program_id(0) == 0)
            def _():
                part_refs[0][...] = part[: tile // 2]
                part_refs[1][...] = part[tile // 2 :]

            @pl.when(pl.program_id(0) == 1)
            def _():
                part_refs[2][...] = part

        if with_input:
            across = (((1,), (1,)), ((), ()))
            term = lax.dot_general(rows_ref[:, :w], weight_refs[0][...], across, preferred_element_type=jnp.float32)
            term += lax.dot_general(rows_ref[:, w:], weight_refs[1][...], across, preferred_element_type=jnp.float32)
            if total_refs:
                term += total_refs[0][...]
            sum_refs[0][...] = term.astype(sum_refs[0].dtype)

    in_specs = [pl.BlockSpec((rows, hidden), lambda i, _: (0, 0), pipeline_mode=pl.Buffered(1))] * count
    operands = [*pieces]
    out_shape, out_specs, scratch = [], [], []
    if count > 1:
        scratch.append(pltpu.VMEM((tokens, hidden), jnp.bfloat16))
    if with_weight:
        in_specs.append(pl.BlockSpec((tile, tokens), lambda i, _: (i, 0)))
        operands.append(input_columns)
        for part_rows in (tile // 2, tile // 2, tile):
            out_shape.append(jax.ShapeDtypeStruct((part_rows, hidden), jnp.bfloat16))
            out_specs.append(pl.BlockSpec((part_rows, hidden), lambda i, _: (0, 0)))
    if with_input:
        in_specs += [pl.BlockSpec((tile, w), lambda i, _: (i, column))] * 2
        operands += [gate_weight, up_weight]
        if total is not None:
            in_specs.append(pl.BlockSpec((tokens, tile), lambda i, _: (0, i)))
            operands.append(total)
        out_shape.append(jax.ShapeDtypeStruct((tokens, width), jnp.bfloat16 if last else jnp.float32))
        out_specs.append(pl.BlockSpec((tokens, tile), lambda i, _: (0, i)))
    return pl.pallas_call(
        kernel,
        out_shape=tuple(out_shape),
        grid_spec=pltpu.PrefetchScalarGridSpec(
            num_scalar_prefetch=1, grid=(TILES,), in_specs=in_specs, out_specs=tuple(out_specs), scratch_shapes=scratch
        ),
        compiler_params=params(),
        cost_estimate=NO_COST,
        name="chunk_grads",
    )(places, *operands)


def body(layer_input, hidden_grad, gate_pre, up_pre, gate_weight, up_weight):
    row, dp = lax.axis_index("row"), lax.axis_index("dp")
    y, z_hi = row // 2, row % 2
    tokens, width = layer_input.shape
    quarter = width // 4
    count = len(CHUNKS)
    steps = jnp.arange(4, dtype=jnp.int32)
    blocks = (y + steps) % 4
    places = jnp.stack([2 * blocks, 2 * blocks + 1], axis=1).reshape(8).astype(jnp.int32)

    swap = lambda value: lax.ppermute(value, "row", ROW_SWAP)
    up = lambda value: lax.ppermute(value, "row", ROW_UP)
    down = lambda value: lax.ppermute(value, "row", ROW_DOWN)
    gather = lambda value: lax.all_gather(value, "row", axis=0, tiled=True, axis_index_groups=SAME_Z)
    own, other, below, above, other_below, other_above, far, other_far, rows = ([None] * count for _ in range(9))

    def grads_of(c):
        s, w, _ = CHUNKS[c]
        return gate_up_grads(*(a[:, s : s + w] for a in (hidden_grad, gate_pre, up_pre)))

    group_input = lax.all_gather(layer_input, "col", axis=0, tiled=True)
    own[0] = grads_of(0)
    other[0] = swap(own[0])
    below[0], above[0] = up(own[0]), down(own[0])
    hidden_grad = after(hidden_grad, own[0])
    for c in range(1, count):
        own[c] = grads_of(c)
    below[2], above[2] = up(own[2]), down(own[2])
    first = (below[0], above[0], other[0])
    other[1] = swap(after(own[1], *first))
    other_0 = after(other[0], *first)
    other_below[0], other_above[0] = up(other_0), down(other_0)
    far[0] = up(after(below[0], *first))
    other[2] = swap(after(own[2], below[2]))
    other[3] = swap(after(own[3], other[1]))
    second = (below[2], above[2], other_below[0], other_above[0])
    other_far[0] = down(after(other_above[0], *second))
    far[2] = up(after(below[2], *second))
    whole_1 = join_rows(steps[:2], after_all([own[1], other[1]], *second))
    rows[1] = gather(whole_1)
    third = (far[0], other_far[0], other[2], other[3])
    input_columns = order_input(after(group_input, *third, whole_1), row, dp)
    other_below[2], other_above[2] = up(other[2]), down(other[2])
    own_3 = after(own[3], other_below[2], other_above[2])
    below[3], above[3] = up(own_3), down(own_3)
    before = [third, (other_below[2], other_above[2]), (), ()]

    inverse_groups = 1.0 / lax.axis_size("dp")
    gate_out = jnp.zeros((quarter, gate_weight.shape[1]), jnp.bfloat16)
    up_out = jnp.zeros((quarter, gate_weight.shape[1]), jnp.bfloat16)
    total = None
    chip_send, pair_parts, finishes = [None] * count, [None] * count, [None] * count
    for c, (s, w, gathered) in enumerate(CHUNKS):
        earlier = [*before[c]]
        if c >= 1:
            earlier += [pair_parts[c - 1], total]
        if c == 1:
            other_far[2] = down(after(other_above[2], chip_send[0]))
            other_3 = after(other[3], below[3], other_far[2])
            other_below[3], other_above[3] = up(other_3), down(other_3)
            far[3], other_far[3] = up(below[3]), down(other_above[3])
            before[2:] = [(above[3], other_below[3], other_above[3]), (far[3], other_far[3])]
        pieces = [rows[c]] if gathered else [
            own[c], other[c], above[c], other_above[c], far[c], other_far[c], below[c], other_below[c]
        ]
        if c == count - 1:
            (input_part,) = chunk_grads(
                places, after_all(pieces, chip_send[c - 1], total), None, gate_weight, up_weight, s, total, True
            )
            gate_out, up_out = after_all([gate_out, up_out], total)
            earlier += [input_part, gate_out, up_out]
        pieces = after_all(pieces, *earlier)
        send_pass, send_stay, keep = chunk_grads(places, pieces, input_columns, None, None, s, None, False)
        core_pass = lax.ppermute(send_pass, "dp", CORE_SWAP)
        core_stay = lax.ppermute(send_stay, "dp", CORE_SWAP)
        chip_send[c] = (keep[:quarter].astype(jnp.float32) + core_pass.astype(jnp.float32)).astype(jnp.bfloat16)
        pair_part = pair_parts[c] = lax.ppermute(chip_send[c], "dp", PAIR_SWAP)
        if c < count - 1:
            pieces = after_all(pieces, chip_send[c])
            (total,) = chunk_grads(places, pieces, None, gate_weight, up_weight, s, total, False)

        def finish(columns, keep=keep, core_stay=core_stay, pair_part=pair_part):
            value = keep[quarter:, columns].astype(jnp.float32) + core_stay[:, columns].astype(jnp.float32)
            return ((value + pair_part[:, columns].astype(jnp.float32)) * inverse_groups).astype(jnp.bfloat16)

        finishes[c] = finish
        for k in ([c - 1] if c else []) + ([c] if c == count - 1 else []):
            start, hidden = CHUNKS[k][:2]
            gate_out = lax.dynamic_update_slice(gate_out, finishes[k](slice(0, hidden)), (0, start))
            up_out = lax.dynamic_update_slice(up_out, finishes[k](slice(hidden, 2 * hidden)), (0, start))

    input_grad = lax.psum_scatter(input_part, "col", scatter_dimension=0, tiled=True)
    halves = input_grad.reshape(2, tokens // 2, width)
    input_grad = jnp.where(z_hi == 0, halves, halves[::-1]).reshape(tokens, width)
    return input_grad, gate_out, up_out


def solution(mesh):
    return jax.shard_map(
        body,
        mesh=mesh,
        in_specs=(
            P(("dp", "col"), "row"),
            P(("dp", "row"), "col"),
            P(("dp", "row"), "col"),
            P(("dp", "row"), "col"),
            P("row", "col"),
            P("row", "col"),
        ),
        out_specs=(P(("dp", "col"), "row"), P(("row", "dp"), "col"), P(("row", "dp"), "col")),
        check_vma=False,
    )
```
